32 devices in a mesh: groups: 2 (over y), rows: 8 (over z, x), hid: 2 (over core).
Axes of the slice: x: 2, y: 2, z: 4, core: 2. Of those that a mesh axis runs over, the one named last changes fastest.
Arguments:
- patches: bfloat16 [128, 6144], P(('groups', 'rows'), 'hid'), parts along dimension 0, may hold values from -6 to 6
- w_up: bfloat16 [6144, 24576], P('hid', 'rows'), may hold values from -0.078125 to 0.078125
- b_up: bfloat16 [24576], P('rows'), may hold values from -3 to 3
Outputs:
- target: bfloat16 [128, 24576], P(('groups', 'hid'), 'rows'), parts along dimension 0
The draws below stay inside these ranges and needn't reach their ends.
There are 2 independent parts, one for each index of `groups`. The reference program is written for one: setup_inputs(seed, part) draws one part's arguments, and reference() takes and returns one part's arrays. A program takes and returns all parts, laid end to end along the dimension named above; an argument that names none is the same for every part. Nothing has to cross between parts.
All inputs are finite; a program needn't handle non-finite values.
Results may differ from the reference program's by a relative error of at most 0.001.
Values may be sent and summed in bfloat16 or wider, within the bound.
A program may use at most 576 MiB of HBM per device.

```python
import jax
import jax.numpy as jnp

D = 6144
FF = 24576
TOKENS = 64


def steps_of(stream_key, shape, pieces, low, top_value):
    def one(dim, blocks):
        draws = jax.random.uniform(jax.random.fold_in(jax.random.fold_in(stream_key, 6), dim), (blocks,), jnp.float32, low / len(pieces), top_value / len(pieces))
        return jnp.repeat(jnp.exp(draws), shape[dim] // blocks).reshape((-1,) + (1,) * (len(shape) - dim - 1))

    level = one(*pieces[0])
    for cut in pieces[1:]:
        level = level * one(*cut)
    return level


def centred(stream_key, shape, deviation, limit, split=(), dtype=jnp.bfloat16):
    result = jax.random.normal(stream_key, shape, jnp.float32) * deviation
    if len(split) > 0:
        result = steps_of(stream_key, shape, split, -0.22, 0.18) * result
    return jnp.clip(result, min=-limit, max=limit).astype(dtype)


def setup_inputs(seed: int = 0, part: int = 0) -> dict:
    arg_keys = jax.random.split(jax.random.key(seed), 4)
    part_splits = jax.random.split(jax.random.fold_in(arg_keys[3], part), 4)
    patches = centred(part_splits[0], (TOKENS, D), 1.0, 6.0, ((0, 8), (1, 2)))
    w_up = centred(arg_keys[1], (D, FF), D ** -0.5, 0.078125, ((0, 2), (1, 8)))
    b_up = centred(arg_keys[2], (FF,), 0.5, 3.0, ((0, 8),))
    return {"patches": patches, "w_up": w_up, "b_up": b_up}


def reference(patches, w_up, b_up):
    pre = jnp.dot(patches, w_up, preferred_element_type=jnp.float32) + b_up.astype(jnp.float32)[None, :]
    return jax.nn.gelu(pre, approximate=False).astype(jnp.bfloat16)
```

```python
import functools

import jax
import jax.numpy as jnp
from jax import lax
from jax.experimental import pallas as pl
from jax.experimental.pallas import tpu as pltpu
from jax.sharding import PartitionSpec as P

MESH = pl.DeviceIdType.MESH


def gelu(value):
    return value * (1.0 + lax.erf(value * (0.5**0.5))) * 0.5


def kernel(shape, p_ref, w_ref, b_ref, o_ref, xg, wv, acc, inc,
           w_sem, own_sem, send_sem, recv_sem, part_send, part_recv):
    lines, pair, k_parts, c_parts = shape
    depth, width = wv.shape[1], acc.shape[-1]
    rows = acc.shape[1] * acc.shape[2]
    me = lax.axis_index("rows")
    half = lax.axis_index("hid")
    line, side = me // pair, lax.rem(me, pair)
    has_up, has_down = line < lines - 1, line > 0
    across = line * pair + (pair - 1 - side)
    up, down = me + pair, me - pair

    weights = [
        pltpu.make_async_copy(w_ref.at[pl.ds(k * depth, depth)], wv.at[k], w_sem.at[k])
        for k in range(k_parts)
    ]
    for copy in weights:
        copy.start()
    mine = [
        pltpu.make_async_copy(p_ref.at[:, pl.ds(k * depth, depth)], xg.at[k, me], own_sem.at[k])
        for k in range(k_parts)
    ]
    for copy in mine:
        copy.start()

    barrier = pltpu.get_barrier_semaphore()
    pl.semaphore_signal(barrier, inc=1, device_id={"hid": 1 - half}, device_id_type=MESH)
    pl.semaphore_signal(barrier, inc=1, device_id={"rows": across}, device_id_type=MESH)

    @pl.when(has_up)
    def _():
        pl.semaphore_signal(barrier, inc=1, device_id={"rows": up}, device_id_type=MESH)

    @pl.when(has_down)
    def _():
        pl.semaphore_signal(barrier, inc=1, device_id={"rows": down}, device_id_type=MESH)

    pl.semaphore_wait(barrier, 2 + has_up.astype(jnp.int32) + has_down.astype(jnp.int32))

    def pass_on(k, block, target, way, own=False):
        source = p_ref.at[:, pl.ds(k * depth, depth)] if own else xg.at[k, block]
        return pltpu.make_async_remote_copy(
            src_ref=source,
            dst_ref=xg.at[k, block],
            send_sem=send_sem.at[k, block, way],
            recv_sem=recv_sem.at[k, block],
            device_id={"rows": target},
            device_id_type=MESH,
        )

    for k in range(k_parts):
        @pl.when(has_up)
        def _():
            pass_on(k, me, up, 0, True).start()

        @pl.when(has_down)
        def _():
            pass_on(k, me, down, 1, True).start()

        pass_on(k, me, across, 2, True).start()

    def stage(k, d):
        @pl.when(line >= d)
        def _():
            block = me - d * pair
            pass_on(k, block, across, 2).wait_recv()

            @pl.when(has_up)
            def _():
                pass_on(k, block, up, 0).start()

            pass_on(k, block, across, 2).start()

        @pl.when(line + d < lines)
        def _():
            block = me + d * pair
            pass_on(k, block, across, 2).wait_recv()

            @pl.when(has_down)
            def _():
                pass_on(k, block, down, 1).start()

            pass_on(k, block, across, 2).start()

    def part_copy(c):
        return pltpu.make_async_remote_copy(
            src_ref=acc.at[c, 1 - half],
            dst_ref=inc.at[c],
            send_sem=part_send.at[c],
            recv_sem=part_recv.at[c],
            device_id={"hid": 1 - half},
            device_id_type=MESH,
        )

    def multiply(k):
        mine[k].wait()
        for other in range(lines):
            block = other * pair + (pair - 1 - side)
            pass_on(k, block, across, 2).wait_recv()
        weights[k].wait()
        x = xg[k].astype(jnp.float32).reshape(rows, depth).astype(jnp.bfloat16)
        for c in range(c_parts):
            product = jnp.dot(
                x, wv[k, :, c * width:(c + 1) * width], preferred_element_type=jnp.float32
            ).reshape(acc.shape[1:])
            if k > 0:
                product = product + acc[c]
            acc[c] = product
            if k == k_parts - 1:
                part_copy(c).start()

    for t in range(1, k_parts + lines + 1):
        for k in range(k_parts):
            if 1 <= t - k < lines:
                stage(k, t - k)
        if 0 <= t - lines < k_parts:
            multiply(t - lines)

    for c in range(c_parts):
        part_copy(c).wait()
        cut = slice(c * width, (c + 1) * width)
        value = acc[c, half] + inc[c] + b_ref[:, cut].astype(jnp.float32)
        o_ref[:, cut] = gelu(value).astype(o_ref.dtype)

    for k in range(k_parts):
        for other in range(lines):
            block = other * pair + side
            pass_on(k, block, across, 2).wait_send()

            @pl.when(jnp.logical_and(has_up, other <= line))
            def _():
                pass_on(k, block, up, 0).wait_send()

            @pl.when(jnp.logical_and(has_down, other >= line))
            def _():
                pass_on(k, block, down, 1).wait_send()


def per_device(patches, w_up, b_up):
    count = lax.axis_size("rows")
    tokens, features = patches.shape
    columns = w_up.shape[1]
    pair = 2
    lines = count // pair
    k_parts = 4 if count <= 8 else 1
    width = 512 if columns % 512 == 0 else columns
    c_parts = columns // width
    depth = features // k_parts
    rows = count * tokens
    out_rows = rows // 2
    any_space = pl.BlockSpec(memory_space=pl.ANY)
    vmem = pl.BlockSpec(memory_space=pltpu.VMEM)
    dma = pltpu.SemaphoreType.DMA
    return pl.pallas_call(
        functools.partial(kernel, (lines, pair, k_parts, c_parts)),
        out_shape=jax.ShapeDtypeStruct((out_rows, columns), jnp.bfloat16),
        in_specs=[any_space, any_space, vmem],
        out_specs=vmem,
        scratch_shapes=[
            pltpu.VMEM((k_parts, count, tokens, depth), jnp.bfloat16),
            pltpu.VMEM((k_parts, depth, columns), jnp.bfloat16),
            pltpu.VMEM((c_parts, 2, out_rows, width), jnp.float32),
            pltpu.VMEM((c_parts, out_rows, width), jnp.float32),
            dma((k_parts,)),
            dma((k_parts,)),
            dma((k_parts, count, 3)),
            dma((k_parts, count)),
            dma((c_parts,)),
            dma((c_parts,)),
        ],
        compiler_params=pltpu.CompilerParams(
            collective_id=0, has_side_effects=True, vmem_limit_bytes=48 * 2**20
        ),
        cost_estimate=pl.CostEstimate(
            flops=2 * rows * features * columns,
            bytes_accessed=2 * features * columns,
            transcendentals=out_rows * columns,
        ),
    )(patches, w_up, b_up.reshape(1, columns))


def solution(mesh):
    return jax.shard_map(
        per_device,
        mesh=mesh,
        in_specs=(P(("groups", "rows"), "hid"), P("hid", "rows"), P("rows")),
        out_specs=P(("groups", "hid"), "rows"),
        check_vma=False,
    )
```

```python
import functools

import jax
import jax.numpy as jnp
from jax import lax
from jax.experimental import pallas as pl
from jax.experimental.pallas import tpu as pltpu
from jax.sharding import PartitionSpec as P

MESH = pl.DeviceIdType.MESH
W,G,X,M = 3,512,1,0
KP, WIDTH, EPI, ORD = W,G,X,M


def gelu(value):
    return value * (1.0 + lax.erf(value * (0.5**0.5))) * 0.5


def kernel(k_parts, c_parts, p_ref, w_ref, *refs):
    b_ref, o_ref, xg, wv, acc, inc, w_sem, send_sem, recv_sem, part_send, part_recv = (
        refs if not EPI else (None,) + refs)
    count, tokens, depth = xg.shape[1:]
    width = acc.shape[-1]
    rows = count * tokens
    me = lax.axis_index("rows")
    half = lax.axis_index("hid")

    def peers(body):
        if count <= 8:
            order = sorted(range(1, count), key=lambda i: abs(i - count // 2)) if ORD == 0 else range(1, count)
            for i in order:
                body(lax.rem(me + i, count))
        else:
            def step(i, carry):
                body(lax.rem(me + i, count))
                return carry
            lax.fori_loop(1, count, step, 0)

    barrier = pltpu.get_barrier_semaphore()
    peers(lambda peer: pl.semaphore_signal(
        barrier, inc=1, device_id={"rows": peer}, device_id_type=MESH))
    pl.semaphore_signal(barrier, inc=1, device_id={"hid": 1 - half}, device_id_type=MESH)

    weights = [
        pltpu.make_async_copy(w_ref.at[pl.ds(k * depth, depth)], wv.at[k], w_sem.at[k])
        for k in range(k_parts)
    ]
    own = [p_ref.at[:, pl.ds(k * depth, depth)] for k in range(k_parts)]
    for k in range(k_parts):
        pltpu.make_async_copy(own[k], xg.at[k, me], recv_sem.at[k]).start()
    for copy in weights:
        copy.start()

    pl.semaphore_wait(barrier, count)

    for k in range(k_parts):
        peers(lambda peer: pltpu.make_async_remote_copy(
            src_ref=own[k],
            dst_ref=xg.at[k, me],
            send_sem=send_sem.at[k],
            recv_sem=recv_sem.at[k],
            device_id={"rows": peer},
            device_id_type=MESH,
        ).start())

    def part_copy(c):
        return pltpu.make_async_remote_copy(
            src_ref=acc.at[c, 1 - half],
            dst_ref=inc.at[c],
            send_sem=part_send.at[c],
            recv_sem=part_recv.at[c],
            device_id={"hid": 1 - half},
            device_id_type=MESH,
        )

    for k in range(k_parts):
        weights[k].wait()
        pltpu.make_async_copy(xg.at[k], xg.at[k], recv_sem.at[k]).wait()
        x = xg[k].astype(jnp.float32).reshape(rows, depth).astype(jnp.bfloat16)
        for c in range(c_parts):
            product = jnp.dot(
                x, wv[k, :, c * width:(c + 1) * width], preferred_element_type=jnp.float32
            ).reshape(acc.shape[1:])
            if k > 0:
                product = product + acc[c]
            acc[c] = product
            if k == k_parts - 1:
                part_copy(c).start()

    for k in range(k_parts):
        sent = xg.at[k, pl.ds(0, count - 1)]
        pltpu.make_async_copy(sent, sent, send_sem.at[k]).wait()

    for c in range(c_parts):
        part_copy(c).wait()
        cut = slice(c * width, (c + 1) * width)
        value = acc[c, half] + inc[c]
        if EPI:
            o_ref[:, cut] = value
        else:
            value = value + b_ref[:, cut].astype(jnp.float32)
            o_ref[:, cut] = gelu(value).astype(o_ref.dtype)


def per_device(patches, w_up, b_up):
    count = lax.axis_size("rows")
    tokens, features = patches.shape
    columns = w_up.shape[1]
    k_parts = KP if count <= 8 else 1
    width = WIDTH if columns % WIDTH == 0 else columns
    c_parts = columns // width
    depth = features // k_parts
    rows = count * tokens
    out_rows = rows // 2
    hbm = pl.BlockSpec(memory_space=pltpu.HBM)
    vmem = pl.BlockSpec(memory_space=pltpu.VMEM)
    dma = pltpu.SemaphoreType.DMA
    result = pl.pallas_call(
        functools.partial(kernel, k_parts, c_parts),
        out_shape=jax.ShapeDtypeStruct((out_rows, columns), jnp.float32 if EPI else jnp.bfloat16),
        in_specs=[hbm, hbm] + ([] if EPI else [vmem]),
        out_specs=vmem,
        scratch_shapes=[
            pltpu.VMEM((k_parts, count, tokens, depth), jnp.bfloat16),
            pltpu.VMEM((k_parts, depth, columns), jnp.bfloat16),
            pltpu.VMEM((c_parts, 2, out_rows, width), jnp.float32),
            pltpu.VMEM((c_parts, out_rows, width), jnp.float32),
            dma((k_parts,)),
            dma((k_parts,)),
            dma((k_parts,)),
            dma((c_parts,)),
            dma((c_parts,)),
        ],
        compiler_params=pltpu.CompilerParams(
            collective_id=0, has_side_effects=True, vmem_limit_bytes=48 * 2**20
        ),
        cost_estimate=pl.CostEstimate(
            flops=2 * rows * features * columns,
            bytes_accessed=2 * features * columns,
            transcendentals=out_rows * columns,
        ),
    )(patches, w_up, *(() if EPI else (b_up.reshape(1, columns),)))
    if not EPI:
        return result
    return gelu(result + b_up.astype(jnp.float32)[None, :]).astype(jnp.bfloat16)


def solution(mesh):
    return jax.shard_map(
        per_device,
        mesh=mesh,
        in_specs=(P(("groups", "rows"), "hid"), P("hid", "rows"), P("rows")),
        out_specs=P(("groups", "hid"), "rows"),
        check_vma=False,
    )
```

```python
import functools

import jax
import jax.numpy as jnp
from jax import lax
from jax.experimental import pallas as pl
from jax.experimental.pallas import tpu as pltpu
from jax.sharding import PartitionSpec as P

MESH = pl.DeviceIdType.MESH
W,G,X,M = 2,512,0,1
KP, WIDTH = W,G


def gelu(value):
    return value * (1.0 + lax.erf(value * (0.5**0.5))) * 0.5


def kernel(k_parts, c_parts, p_ref, w_ref, b_ref, o_ref, xg, wv, bv, acc, inc,
           w_sem, b_sem, send_sem, recv_sem, part_send, part_recv):
    count, tokens, depth = xg.shape[1:]
    width = acc.shape[-1]
    rows = count * tokens
    me = lax.axis_index("rows")
    half = lax.axis_index("hid")

    def peers(body):
        if count <= 8:
            for i in range(1, count):
                body(lax.rem(me + i, count))
        else:
            def step(i, carry):
                body(lax.rem(me + i, count))
                return carry
            lax.fori_loop(1, count, step, 0)

    barrier = pltpu.get_barrier_semaphore()
    peers(lambda peer: pl.semaphore_signal(
        barrier, inc=1, device_id={"rows": peer}, device_id_type=MESH))
    pl.semaphore_signal(barrier, inc=1, device_id={"hid": 1 - half}, device_id_type=MESH)

    weights = [
        pltpu.make_async_copy(w_ref.at[pl.ds(k * depth, depth)], wv.at[k], w_sem.at[k])
        for k in range(k_parts)
    ]
    own = [p_ref.at[:, pl.ds(k * depth, depth)] for k in range(k_parts)]
    for k in range(k_parts):
        pltpu.make_async_copy(own[k], xg.at[k, me], recv_sem.at[k]).start()
    bias = pltpu.make_async_copy(b_ref, bv, b_sem)
    for copy in weights + [bias]:
        copy.start()

    pl.semaphore_wait(barrier, count)

    for k in range(k_parts):
        peers(lambda peer: pltpu.make_async_remote_copy(
            src_ref=own[k],
            dst_ref=xg.at[k, me],
            send_sem=send_sem.at[k],
            recv_sem=recv_sem.at[k],
            device_id={"rows": peer},
            device_id_type=MESH,
        ).start())

    def part_copy(c):
        return pltpu.make_async_remote_copy(
            src_ref=acc.at[c, 1 - half],
            dst_ref=inc.at[c],
            send_sem=part_send.at[c],
            recv_sem=part_recv.at[c],
            device_id={"hid": 1 - half},
            device_id_type=MESH,
        )

    for k in range(k_parts):
        weights[k].wait()
        pltpu.make_async_copy(xg.at[k], xg.at[k], recv_sem.at[k]).wait()
        x = xg[k].astype(jnp.float32).reshape(rows, depth).astype(jnp.bfloat16)
        for c in range(c_parts):
            product = jnp.dot(
                x, wv[k, :, c * width:(c + 1) * width], preferred_element_type=jnp.float32
            ).reshape(acc.shape[1:])
            if k > 0:
                product = product + acc[c]
            acc[c] = product
            if k == k_parts - 1:
                part_copy(c).start()

    for k in range(k_parts):
        sent = xg.at[k, pl.ds(0, count - 1)]
        pltpu.make_async_copy(sent, sent, send_sem.at[k]).wait()

    bias.wait()
    for c in range(c_parts):
        part_copy(c).wait()
        cut = slice(c * width, (c + 1) * width)
        value = acc[c, half] + inc[c] + bv[cut].astype(jnp.float32).reshape(1, width)
        o_ref[:, cut] = gelu(value).astype(o_ref.dtype)


def per_device(patches, w_up, b_up):
    count = lax.axis_size("rows")
    tokens, features = patches.shape
    columns = w_up.shape[1]
    k_parts = KP if count <= 8 else 1
    width = WIDTH if columns % WIDTH == 0 else columns
    c_parts = columns // width
    depth = features // k_parts
    rows = count * tokens
    out_rows = rows // 2
    hbm = pl.BlockSpec(memory_space=pltpu.HBM)
    dma = pltpu.SemaphoreType.DMA
    return pl.pallas_call(
        functools.partial(kernel, k_parts, c_parts),
        out_shape=jax.ShapeDtypeStruct((out_rows, columns), jnp.bfloat16),
        in_specs=[hbm, hbm, hbm],
        out_specs=pl.BlockSpec(memory_space=pltpu.VMEM),
        scratch_shapes=[
            pltpu.VMEM((k_parts, count, tokens, depth), jnp.bfloat16),
            pltpu.VMEM((k_parts, depth, columns), jnp.bfloat16),
            pltpu.VMEM((columns,), jnp.bfloat16),
            pltpu.VMEM((c_parts, 2, out_rows, width), jnp.float32),
            pltpu.VMEM((c_parts, out_rows, width), jnp.float32),
            dma((k_parts,)),
            dma,
            dma((k_parts,)),
            dma((k_parts,)),
            dma((c_parts,)),
            dma((c_parts,)),
        ],
        compiler_params=pltpu.CompilerParams(
            collective_id=0, has_side_effects=True, vmem_limit_bytes=48 * 2**20
        ),
        cost_estimate=pl.CostEstimate(
            flops=2 * rows * features * columns,
            bytes_accessed=2 * features * columns,
            transcendentals=out_rows * columns,
        ),
    )(*(pltpu.with_memory_space_constraint(a, pltpu.HBM) for a in (patches, w_up, b_up)))


def solution(mesh):
    return jax.shard_map(
        per_device,
        mesh=mesh,
        in_specs=(P(("groups", "rows"), "hid"), P("hid", "rows"), P("rows")),
        out_specs=P(("groups", "hid"), "rows"),
        check_vma=False,
    )
```

```python
import functools

import jax
import jax.numpy as jnp
from jax import lax
from jax.experimental import pallas as pl
from jax.experimental.pallas import tpu as pltpu
from jax.sharding import PartitionSpec as P

MESH = pl.DeviceIdType.MESH
KP, WIDTH = 2, 1024


def gelu(value):
    return value * (1.0 + lax.erf(value * (0.5**0.5))) * 0.5


def kernel(k_parts, c_parts, p_ref, w_ref, b_ref, o_ref, xg, wv, bv, acc, inc,
           w_sem, b_sem, send_sem, recv_sem, part_send, part_recv):
    count, tokens, depth = xg.shape[1:]
    width = acc.shape[-1]
    rows = count * tokens
    me = lax.axis_index("rows")
    half = lax.axis_index("hid")

    def peers(body):
        if count <= 8:
            for i in range(1, count):
                body(lax.rem(me + i, count))
        else:
            def step(i, carry):
                body(lax.rem(me + i, count))
                return carry
            lax.fori_loop(1, count, step, 0)

    barrier = pltpu.get_barrier_semaphore()
    peers(lambda peer: pl.semaphore_signal(
        barrier, inc=1, device_id={"rows": peer}, device_id_type=MESH))
    pl.semaphore_signal(barrier, inc=1, device_id={"hid": 1 - half}, device_id_type=MESH)

    weights = [
        pltpu.make_async_copy(w_ref.at[pl.ds(k * depth, depth)], wv.at[k], w_sem.at[k])
        for k in range(k_parts)
    ]
    own = [p_ref.at[:, pl.ds(k * depth, depth)] for k in range(k_parts)]
    for k in range(k_parts):
        pltpu.make_async_copy(own[k], xg.at[k, me], recv_sem.at[k]).start()
    bias = pltpu.make_async_copy(b_ref, bv, b_sem)
    for copy in weights + [bias]:
        copy.start()

    pl.semaphore_wait(barrier, count)

    for k in range(k_parts):
        peers(lambda peer: pltpu.make_async_remote_copy(
            src_ref=own[k],
            dst_ref=xg.at[k, me],
            send_sem=send_sem.at[k],
            recv_sem=recv_sem.at[k],
            device_id={"rows": peer},
            device_id_type=MESH,
        ).start())

    def part_copy(c):
        return pltpu.make_async_remote_copy(
            src_ref=acc.at[c, 1 - half],
            dst_ref=inc.at[c],
            send_sem=part_send.at[c],
            recv_sem=part_recv.at[c],
            device_id={"hid": 1 - half},
            device_id_type=MESH,
        )

    for k in range(k_parts):
        weights[k].wait()
        pltpu.make_async_copy(xg.at[k], xg.at[k], recv_sem.at[k]).wait()
        x = xg[k].astype(jnp.float32).reshape(rows, depth).astype(jnp.bfloat16)
        for c in range(c_parts):
            product = jnp.dot(
                x, wv[k, :, c * width:(c + 1) * width], preferred_element_type=jnp.float32
            ).reshape(acc.shape[1:])
            if k > 0:
                product = product + acc[c]
            acc[c] = product
            if k == k_parts - 1:
                part_copy(c).start()

    for k in range(k_parts):
        sent = xg.at[k, pl.ds(0, count - 1)]
        pltpu.make_async_copy(sent, sent, send_sem.at[k]).wait()

    bias.wait()
    for c in range(c_parts):
        part_copy(c).wait()
        cut = slice(c * width, (c + 1) * width)
        value = acc[c, half] + inc[c] + bv[cut].astype(jnp.float32).reshape(1, width)
        o_ref[:, cut] = gelu(value).astype(o_ref.dtype)


def per_device(patches, w_up, b_up):
    count = lax.axis_size("rows")
    tokens, features = patches.shape
    columns = w_up.shape[1]
    k_parts = KP if count <= 8 else 1
    width = WIDTH if columns % WIDTH == 0 else columns
    c_parts = columns // width
    depth = features // k_parts
    rows = count * tokens
    out_rows = rows // 2
    hbm = pl.BlockSpec(memory_space=pltpu.HBM)
    dma = pltpu.SemaphoreType.DMA
    return pl.pallas_call(
        functools.partial(kernel, k_parts, c_parts),
        out_shape=jax.ShapeDtypeStruct((out_rows, columns), jnp.bfloat16),
        in_specs=[hbm, hbm, hbm],
        out_specs=pl.BlockSpec(memory_space=pltpu.VMEM),
        scratch_shapes=[
            pltpu.VMEM((k_parts, count, tokens, depth), jnp.bfloat16),
            pltpu.VMEM((k_parts, depth, columns), jnp.bfloat16),
            pltpu.VMEM((columns,), jnp.bfloat16),
            pltpu.VMEM((c_parts, 2, out_rows, width), jnp.float32),
            pltpu.VMEM((c_parts, out_rows, width), jnp.float32),
            dma((k_parts,)),
            dma,
            dma((k_parts,)),
            dma((k_parts,)),
            dma((c_parts,)),
            dma((c_parts,)),
        ],
        compiler_params=pltpu.CompilerParams(
            collective_id=0, has_side_effects=True, vmem_limit_bytes=48 * 2**20
        ),
        cost_estimate=pl.CostEstimate(
            flops=2 * rows * features * columns,
            bytes_accessed=2 * features * columns,
            transcendentals=out_rows * columns,
        ),
    )(*(pltpu.with_memory_space_constraint(a, pltpu.HBM) for a in (patches, w_up, b_up)))


def solution(mesh):
    return jax.shard_map(
        per_device,
        mesh=mesh,
        in_specs=(P(("groups", "rows"), "hid"), P("hid", "rows"), P("rows")),
        out_specs=P(("groups", "hid"), "rows"),
        check_vma=False,
    )
```
